32 devices in a mesh: tm: 8 (over z, y), sub: 4 (over x, core).
Axes of the slice: x: 2, y: 2, z: 4, core: 2. Of those that a mesh axis runs over, the one named last changes fastest.
Arguments:
- frames: bfloat16 [8192, 1024], P(('tm', 'sub')), may hold values from -16 to 16
- modulation: float32 [8, 1024], replicated, may hold values from -4 to 4
- w_project: bfloat16 [3, 1024, 1024], P(None, None, 'sub'), may hold values from -1 to 1
- w_heads_out: bfloat16 [1024, 1024], P('sub'), may hold values from -0.25 to 0.25
- w_up: bfloat16 [1024, 4096], P(None, 'sub'), may hold values from -0.1875 to 0.1875
- w_down: bfloat16 [4096, 1024], P('sub'), may hold values from -0.125 to 0.125
- w_velocity: bfloat16 [1024, 100], replicated, may hold values from -0.1875 to 0.1875
- noisy_mel: float32 [8192, 100], P('tm'), may hold values from -6 to 6
- w_prelude: bfloat16 [7, 1536, 100], P(None, 'sub'), may hold values from -0.21875 to 0.21875
- w_upsample: bfloat16 [8, 1536, 768], P(None, 'sub'), may hold values from -0.109375 to 0.109375
- snake_alpha: float32 [2, 768], replicated, may hold values from 0.3 to 3
- w_dilated: bfloat16 [3, 768, 768], P(None, 'sub'), may hold values from -0.125 to 0.125
- w_plain: bfloat16 [3, 768, 768], P(None, 'sub'), may hold values from -0.125 to 0.125
Outputs:
- mel_next: float32 [8192, 100], P('tm')
- section_out: bfloat16 [32768, 768], P(('tm', 'sub'))
The draws below stay inside these ranges and needn't reach their ends.
All inputs are finite; a program needn't handle non-finite values.
Results may differ from the reference program's by a relative error of at most 0.03.
Values may be sent and summed in bfloat16 or wider, within the bound.
A program may use at most 64 MiB of HBM per device.

```python
import math
import jax
import jax.numpy as jnp
from jax import lax

D = 1024
HEADS = 16
HEAD_DIM = 64
FF = 4096
MEL = 100
C_IN = 1536
C_MID = 768
BLK = 256
FRAMES = 8192
N_SUB = 4


def draw_frames(key, part):
    own_key = jax.random.fold_in(key, 11)
    entries = jax.random.normal(jax.random.fold_in(own_key, 1), (FRAMES, D), jnp.float32)
    drawn = entries
    return jnp.clip(drawn, -16.0, 16.0).astype(jnp.bfloat16)


def draw_w_project(key, part):
    own_key = jax.random.fold_in(key, 12)
    drawn = jnp.clip(jax.random.normal(jax.random.fold_in(own_key, 2), (3, D, D), jnp.float32), -6.0, 6.0) / math.sqrt(D)
    return jnp.clip(drawn, -1.0, 1.0).astype(jnp.bfloat16)


def strengthened(values, stream_key, source, target, shards_of, factor):
    owner, partner = [(jnp.arange(values.shape[axis_at]) // (values.shape[axis_at] // shards_of)).reshape([-1 if axis == axis_at else 1 for axis in range(values.ndim)]) for axis_at in (source, target)]
    chosen = jax.random.permutation(stream_key, shards_of)[partner]
    strong = (owner == chosen) | (owner == (partner + shards_of // 2) % shards_of)
    return jnp.where(strong, factor * values, values)


def shard_levels(key, dims, pieces, low, top_value):
    gain, own = 1.0, jax.random.fold_in(key, 6)
    for axis_at, shards_of in pieces:
        heights = jnp.exp(jax.random.uniform(jax.random.fold_in(own, axis_at), (shards_of,), jnp.float32, low / len(pieces), top_value / len(pieces)))
        gain = gain * jnp.repeat(heights, dims[axis_at] // shards_of).reshape([-1 if axis == axis_at else 1 for axis in range(len(dims))])
    return gain


def gaussian(stream_key, dims, scale, reach, shards=(), held_as=jnp.bfloat16):
    factor_of = shard_levels(stream_key, dims, shards, -0.22, 0.18) if shards else 1.0
    values = jax.random.normal(stream_key, dims, jnp.float32) * scale * factor_of
    return jnp.minimum(jnp.maximum(values, -reach), reach).astype(held_as)


def noise_with(rng, shape, width, reach, split, heavy, held_as=jnp.bfloat16):
    values = width * jax.random.normal(rng, shape, jnp.float32)
    if split:
        values = values * shard_levels(rng, shape, split, -0.22, 0.18)
    return jnp.clip(strengthened(values, jax.random.fold_in(rng, 3), *heavy), -reach, reach).astype(held_as)


def setup_inputs(seed: int = 0) -> dict:
    streams_of = jax.random.split(jax.random.key(seed), 14)
    return {
        "frames": draw_frames(jax.random.fold_in(streams_of[13], 71), 0),
        "modulation": gaussian(streams_of[1], (8, D), 1.0, 4.0, (), jnp.float32),
        "w_project": draw_w_project(jax.random.fold_in(streams_of[13], 71), 0),
        "w_heads_out": noise_with(streams_of[3], (D, D), D ** -0.5, 0.25, ((0, 4),), (0, 1, 4, 2.0)),
        "w_up": gaussian(streams_of[4], (D, FF), D ** -0.5, 0.1875, ((1, 4),)),
        "w_down": noise_with(streams_of[5], (FF, D), FF ** -0.5, 0.125, ((0, 4),), (0, 1, 4, 2.0)),
        "w_velocity": gaussian(streams_of[6], (D, MEL), D ** -0.5, 0.1875),
        "noisy_mel": gaussian(streams_of[7], (FRAMES, MEL), 1.0, 6.0, ((0, 8),), jnp.float32),
        "w_prelude": gaussian(streams_of[8], (7, C_IN, MEL), (7 * MEL) ** -0.5, 0.21875, ((1, 4),)),
        "w_upsample": gaussian(streams_of[9], (8, C_IN, C_MID), (2 * C_IN) ** -0.5, 0.109375, ((1, 4),)),
        "snake_alpha": jnp.clip(jnp.exp(jax.random.uniform(streams_of[10], (2, C_MID), jnp.float32, math.log(0.3), math.log(3.0))), 0.3, 3.0),
        "w_dilated": gaussian(streams_of[11], (3, C_MID, C_MID), (3 * C_MID) ** -0.5, 0.125, ((1, 4),)),
        "w_plain": gaussian(streams_of[12], (3, C_MID, C_MID), (3 * C_MID) ** -0.5, 0.125, ((1, 4),)),
    }


epsilon = 1e-06

def norm_rows(rows, offset_row, scale_row):
    rows = rows.astype(jnp.float32)
    center = lax.optimization_barrier(jnp.mean(rows, axis=-1, keepdims=True))
    square = lax.optimization_barrier(jnp.mean(rows * rows, axis=-1, keepdims=True))
    spread = square - center * center
    return (rows - center) * lax.rsqrt(spread + epsilon) * (1.0 + scale_row) + offset_row

def snake_act(values, alpha_row):
    return values + jnp.square(jnp.sin(alpha_row * values)) / alpha_row

def settle(values):
    return lax.optimization_barrier(values.astype(jnp.bfloat16)).astype(jnp.float32)

def grouped_product(left, right, groups):
    group_width = left.shape[1] // groups

    def add_group(group_index, running):
        first_col = (group_index * group_width).astype(jnp.int32)
        part_left = lax.dynamic_slice_in_dim(left, first_col, group_width, 1)
        part_right = lax.dynamic_slice_in_dim(right, first_col, group_width, 0)
        return running + settle(jnp.dot(part_left, part_right, preferred_element_type=jnp.float32))
    empty_sum = jnp.zeros((left.shape[0], right.shape[1]), jnp.float32)
    return lax.fori_loop(0, groups, add_group, empty_sum)

def block_attention(queries, keys_now, values_now):
    blocks = FRAMES // BLK
    block_shape = (blocks, BLK, HEADS, HEAD_DIM)
    query_blocks = queries.reshape(block_shape)
    key_blocks = keys_now.reshape(block_shape)
    value_blocks = values_now.reshape(block_shape)
    empty_block = jnp.zeros((1, BLK, HEADS, HEAD_DIM), jnp.bfloat16)
    key_all = jnp.concatenate([jnp.concatenate([empty_block, key_blocks[:-1]], 0), key_blocks], 1)
    value_all = jnp.concatenate([jnp.concatenate([empty_block, value_blocks[:-1]], 0), value_blocks], 1)
    leading = jnp.arange(blocks) == 0

    def one_block(inputs):
        query_one, key_one, value_one, is_lead = inputs
        scores = jnp.einsum('qhd,khd->hqk', query_one.astype(jnp.float32), key_one.astype(jnp.float32)) / math.sqrt(HEAD_DIM)
        allowed = jnp.logical_or(jnp.logical_not(is_lead), jnp.arange(2 * BLK) >= BLK)
        scores = jnp.where(allowed[None, None, :], scores, -1e+30)
        largest = lax.optimization_barrier(jnp.max(scores, axis=-1, keepdims=True))
        raised = jnp.exp(scores - largest)
        weights = (raised / lax.optimization_barrier(jnp.sum(raised, axis=-1, keepdims=True))).astype(jnp.bfloat16)
        attended = jnp.einsum('hqk,khd->qhd', weights.astype(jnp.float32), value_one.astype(jnp.float32))
        return attended.astype(jnp.bfloat16)
    attended = lax.map(one_block, (query_blocks, key_all, value_all, leading))
    return attended.reshape((FRAMES, D))

def upsample(prelude, w_upsample):
    group_width = C_IN // N_SUB
    padded = jnp.pad(prelude, ((1, 1), (0, 0)))

    def add_group(group_index, running):
        first_col = (group_index * group_width).astype(jnp.int32)
        part_left = lax.dynamic_slice_in_dim(padded, first_col, group_width, 1)
        tap_weights = lax.dynamic_slice_in_dim(w_upsample, first_col, group_width, 1)
        current = part_left[1:-1]
        earlier = part_left[:-2]
        later_frames = part_left[2:]

        def tap_product(source, offset):
            return jnp.dot(source, tap_weights[offset], preferred_element_type=jnp.float32)
        phases = jnp.stack([tap_product(current, 2) + tap_product(earlier, 6), tap_product(current, 3) + tap_product(earlier, 7), tap_product(current, 4) + tap_product(later_frames, 0), tap_product(current, 5) + tap_product(later_frames, 1)], 1)
        return running + settle(phases.reshape((4 * FRAMES, C_MID)))
    empty_sum = jnp.zeros((4 * FRAMES, C_MID), jnp.float32)
    return lax.fori_loop(0, N_SUB, add_group, empty_sum).astype(jnp.bfloat16)

def kernel_conv(source, weight, gap):
    length = source.shape[0]
    padded = jnp.pad(source, ((gap, gap), (0, 0)))
    running = jnp.zeros((length, weight.shape[2]), jnp.float32)
    for offset in range(3):
        running = running + jnp.dot(padded[offset * gap:offset * gap + length], weight[offset], preferred_element_type=jnp.float32)
    return running

def reference(frames, modulation, w_project, w_heads_out, w_up, w_down, w_velocity, noisy_mel, w_prelude, w_upsample, snake_alpha, w_dilated, w_plain):
    first_norm = norm_rows(frames, modulation[0], modulation[1]).astype(jnp.bfloat16)
    queries = jnp.dot(first_norm, w_project[0], preferred_element_type=jnp.float32).astype(jnp.bfloat16)
    keys_now = jnp.dot(first_norm, w_project[1], preferred_element_type=jnp.float32).astype(jnp.bfloat16)
    values_now = jnp.dot(first_norm, w_project[2], preferred_element_type=jnp.float32).astype(jnp.bfloat16)
    heads_out = block_attention(queries, keys_now, values_now)
    attn = grouped_product(heads_out, w_heads_out, N_SUB)
    mixed_rows = (frames.astype(jnp.float32) + modulation[2] * attn).astype(jnp.bfloat16)
    second_norm = norm_rows(mixed_rows, modulation[3], modulation[4]).astype(jnp.bfloat16)
    hidden = jax.nn.gelu(jnp.dot(second_norm, w_up, preferred_element_type=jnp.float32), approximate=True).astype(jnp.bfloat16)
    feed = grouped_product(hidden, w_down, N_SUB)
    final_rows = (mixed_rows.astype(jnp.float32) + modulation[5] * feed).astype(jnp.bfloat16)
    final_norm = norm_rows(final_rows, modulation[6], modulation[7]).astype(jnp.bfloat16)
    velocity = jnp.dot(final_norm, w_velocity, preferred_element_type=jnp.float32)
    mel_next = noisy_mel + 0.5 * velocity
    mel_low = mel_next.astype(jnp.bfloat16)
    padded = jnp.pad(mel_low, ((3, 3), (0, 0)))
    prelude = jnp.zeros((FRAMES, C_IN), jnp.float32)
    for offset in range(7):
        prelude = prelude + jnp.dot(padded[offset:offset + FRAMES], w_prelude[offset].T, preferred_element_type=jnp.float32)
    prelude = prelude.astype(jnp.bfloat16)
    up_x = upsample(prelude, w_upsample)
    act_one = snake_act(up_x.astype(jnp.float32), snake_alpha[0]).astype(jnp.bfloat16)
    inner_conv = kernel_conv(act_one, w_dilated, 3)
    act_two = snake_act(inner_conv, snake_alpha[1]).astype(jnp.bfloat16)
    outer_conv = kernel_conv(act_two, w_plain, 1)
    section_out = (up_x.astype(jnp.float32) + outer_conv).astype(jnp.bfloat16)
    return (mel_next, section_out)
```

```python
import functools
import math

import jax
import jax.numpy as jnp
from jax import lax
from jax.experimental import pallas as pl
from jax.experimental.pallas import tpu as pltpu
from jax.sharding import PartitionSpec as P

HEAD_DIM = 64
BLK = 256
EPSILON = 1e-06
MESH = pl.DeviceIdType.MESH
VMEM = pltpu.VMEM
DMA = pltpu.SemaphoreType.DMA
F32 = jnp.float32
BF16 = jnp.bfloat16


def norm_rows(rows, offset_row, scale_row):
    center = jnp.mean(rows, axis=-1, keepdims=True)
    square = jnp.mean(rows * rows, axis=-1, keepdims=True)
    spread = square - center * center
    return (rows - center) * lax.rsqrt(spread + EPSILON) * (1.0 + scale_row) + offset_row


def sin_squared(values):
    turns = jnp.round(values * (1.0 / math.pi))
    rest = values - turns * 3.140625
    rest = rest - turns * 9.670257568359375e-04
    rest = rest - turns * 6.2783295e-07
    rest = jnp.clip(rest, -0.5 * math.pi - 1e-3, 0.5 * math.pi + 1e-3)
    u = rest * rest
    series = -1.0 / 39916800.0
    for coefficient in (1.0 / 362880.0, -1.0 / 5040.0, 1.0 / 120.0, -1.0 / 6.0, 1.0):
        series = series * u + coefficient
    return u * series * series


def snake_act(values, alpha_row):
    return values + sin_squared(alpha_row * values) * (1.0 / alpha_row)


def dot(left, right):
    return jnp.dot(left, right, preferred_element_type=F32)


def dot_t(left, right):
    return lax.dot_general(left, right, (((1,), (1,)), ((), ())), preferred_element_type=F32)


class Place:
    def __init__(self):
        self.s = lax.axis_index("sub")
        self.t = lax.axis_index("tm")
        self.n = lax.axis_size("sub")
        self.times = lax.axis_size("tm")
        self.chips = self.n // 2
        self.core = lax.rem(self.s, 2)
        self.chip = self.s // 2
        self.sibling = self.s + 1 - 2 * self.core

    def chip_behind(self, i):
        return lax.rem(self.chip + self.chips - i, self.chips)

    def block(self, i, other_core):
        core = 1 - self.core if other_core else self.core
        return self.chip_behind(i) * 2 + core

    def peer(self, chip):
        return {"sub": chip * 2 + self.core}


def remote(src, dst, send, recv, device):
    return pltpu.make_async_remote_copy(
        src_ref=src, dst_ref=dst, send_sem=send, recv_sem=recv, device_id=device, device_id_type=MESH
    )


def rows_of(block, rows):
    return pl.ds(pl.multiple_of(block * rows, rows), rows)


class Gather:
    def __init__(self, here, buf, rows, sems):
        self.here, self.buf, self.rows = here, buf, rows
        self.x_send, self.x_recv, self.d_send, self.d_recv = sems

    def piece(self, block):
        return self.buf.at[rows_of(block, self.rows)]

    def across(self, i):
        here = self.here
        ahead = lax.rem(here.chip + i, here.chips)
        own = self.piece(here.s)
        return remote(own, own, self.x_send.at[i], self.x_recv.at[i], here.peer(ahead))

    def arriving(self, i):
        own = self.piece(self.here.block(i, False))
        return remote(own, own, self.x_send.at[i], self.x_recv.at[i], self.here.peer(self.here.chip_behind(i)))

    def forward(self, i):
        own = self.piece(self.here.block(i, False))
        return remote(own, own, self.d_send.at[i], self.d_recv.at[i], {"sub": self.here.sibling})

    def start(self):
        for i in range(1, self.here.chips):
            self.across(i).start()
        self.forward(0).start()

    def finish(self):
        for i in range(1, self.here.chips):
            self.across(i).wait_send()
        for i in range(self.here.chips):
            self.forward(i).wait_send()

    def each(self, work):
        here = self.here
        work(here.block(0, False), 0, False)
        self.take_other(0)
        work(here.block(0, True), 0, True)

        def step(i, carry):
            self.arriving(i).wait_recv()
            self.forward(i).start()
            work(here.block(i, False), i, False)
            self.take_other(i)
            work(here.block(i, True), i, True)
            return carry

        lax.fori_loop(1, here.chips, step, 0)

    def take_other(self, i):
        own = self.piece(self.here.block(i, True))
        remote(own, own, self.d_send.at[i], self.d_recv.at[i], {"sub": self.here.sibling}).wait_recv()


class Scatter:
    def __init__(self, here, buf, rows, near, far, sems):
        self.here, self.buf, self.rows, self.near, self.far = here, buf, rows, near, far
        self.a_send, self.a_recv, self.b_send, self.b_recv = sems

    def piece(self, block):
        return self.buf.at[rows_of(block, self.rows)]

    def to_sibling(self, i):
        here = self.here
        return remote(
            self.piece(here.block(i, True)), self.near.at[i], self.a_send.at[i], self.a_recv.at[i],
            {"sub": here.sibling},
        )

    def to_chip(self, i):
        here = self.here
        return remote(
            self.piece(here.block(i, False)), self.far.at[i], self.b_send.at[i], self.b_recv.at[i],
            here.peer(here.chip_behind(i)),
        )

    def pass_on(self, i):
        self.to_sibling(i).wait_recv()
        here, rows = self.here, self.rows
        base = here.block(i, False) * rows
        step = min(64, rows)

        def add(q, carry):
            at = pl.ds(pl.multiple_of(base + q * step, step), step)
            near_at = pl.ds(pl.multiple_of(q * step, step), step)
            self.buf[at] = (self.buf[at].astype(F32) + self.near[i, near_at].astype(F32)).astype(BF16)
            return carry

        lax.fori_loop(0, rows // step, add, 0)
        self.to_chip(i).start()

    def arrive(self):
        self.to_sibling(0).wait_recv()
        for i in range(1, self.here.chips):
            self.to_chip(i).wait_recv()

    def total(self, at):
        start, size = at
        own = pl.ds(pl.multiple_of(self.here.s * self.rows + start, size), size)
        part = pl.ds(pl.multiple_of(start, size), size)
        total = self.buf[own].astype(F32) + self.near[0, part].astype(F32)
        for i in range(1, self.here.chips):
            total = total + self.far[i, part].astype(F32)
        return total

    def finish(self):
        for i in range(self.here.chips):
            self.to_sibling(i).wait_send()
        for i in range(1, self.here.chips):
            self.to_chip(i).wait_send()


def greet(here, extra=()):
    barrier = pltpu.get_barrier_semaphore()
    for i in range(1, here.chips):
        ahead = lax.rem(here.chip + i, here.chips)
        pl.semaphore_signal(barrier, inc=1, device_id=here.peer(ahead), device_id_type=MESH)
    pl.semaphore_signal(barrier, inc=1, device_id={"sub": here.sibling}, device_id_type=MESH)
    for condition, device in extra:

        @pl.when(condition)
        def _():
            pl.semaphore_signal(barrier, inc=1, device_id=device, device_id_type=MESH)

    greeted = here.chips
    for condition, device in extra:
        greeted = greeted + condition.astype(jnp.int32)
    pl.semaphore_wait(barrier, greeted)


def layer_kernel(
    frames, mod, w_project, w_heads_out, w_up, w_down, w_velocity, noisy, mel_out,
    h_one, h_two, queries, keys, values, attended, sums_one, sums_two, near_one, far_one, near_two,
    far_two, mixed, mel_all, gather_sems, scatter_sems, look_send, look_recv,
):
    here = Place()
    rows, width = frames.shape
    total_rows = here.n * rows
    step = min(64, rows)
    steps = rows // step
    first, last = here.t == 0, here.t == here.times - 1
    behind, ahead = {"tm": here.t - 1}, {"tm": here.t + 1}
    greet(here, ((here.t > 0, behind), (here.t < here.times - 1, ahead)))

    def at_step(q, base=0):
        return pl.ds(pl.multiple_of(base + q * step, step), step)

    def norm_one(q, carry):
        out = norm_rows(frames[at_step(q)].astype(F32), mod[0:1], mod[1:2])
        h_one[at_step(q, here.s * rows)] = out.astype(BF16)
        return carry

    lax.fori_loop(0, steps, norm_one, 0)
    gather = Gather(here, h_one, rows, [gather_sems.at[0, j] for j in range(4)])
    gather.start()

    def project(block, i, other):
        at = rows_of(block, rows)
        later = pl.ds(pl.multiple_of(BLK + block * rows, math.gcd(BLK, rows)), rows)
        h = h_one[at]
        queries[at] = (dot(h, w_project[0]).astype(BF16).astype(F32) * (1.0 / math.sqrt(HEAD_DIM))).astype(BF16)
        keys[later] = dot(h, w_project[1]).astype(BF16)
        values[later] = dot(h, w_project[2]).astype(BF16)

    gather.each(project)

    def lookback(buf, j):
        return remote(
            buf.at[pl.ds(total_rows, BLK)], buf.at[pl.ds(0, BLK)], look_send.at[j], look_recv.at[j], ahead
        )

    @pl.when(jnp.logical_not(last))
    def _():
        lookback(keys, 0).start()
        lookback(values, 1).start()

    @pl.when(first)
    def _():
        keys[pl.ds(0, BLK)] = jnp.zeros((BLK, keys.shape[1]), BF16)
        values[pl.ds(0, BLK)] = jnp.zeros((BLK, values.shape[1]), BF16)

    blocks = total_rows // BLK
    heads = queries.shape[1] // HEAD_DIM

    def attend(turn, carry):
        b = lax.rem(turn + 1, blocks)

        @pl.when(jnp.logical_and(b == 0, jnp.logical_not(first)))
        def _():
            lookback(keys, 0).wait_recv()
            lookback(values, 1).wait_recv()

        at = rows_of(b, BLK)
        both = pl.ds(pl.multiple_of(b * BLK, BLK), 2 * BLK)
        key_ids = lax.broadcasted_iota(jnp.int32, (1, 2 * BLK), 1)
        hidden_keys = jnp.where((key_ids < BLK) & (b == 0) & first, -1e30, 0.0)
        for head in range(heads):
            cols = slice(head * HEAD_DIM, (head + 1) * HEAD_DIM)
            scores = dot_t(queries[at, cols], keys[both, cols]) + hidden_keys
            raised = jnp.exp(scores - jnp.max(scores, axis=-1, keepdims=True))
            scale = 1.0 / jnp.sum(raised, axis=-1, keepdims=True)
            attended[:, cols] = (dot(raised.astype(BF16), values[both, cols]) * scale).astype(BF16)
        sums_one[at] = dot(attended[...], w_heads_out[...]).astype(BF16)
        return carry

    lax.fori_loop(0, blocks, attend, 0)

    scatter = Scatter(here, sums_one, rows, near_one, far_one, [scatter_sems.at[0, j] for j in range(4)])
    for i in reversed(range(here.chips)):
        scatter.to_sibling(i).start()
    for i in range(1, here.chips):
        scatter.pass_on(i)
    scatter.arrive()

    def norm_two(q, carry):
        attn = scatter.total((q * step, step))
        mix = (frames[at_step(q)].astype(F32) + mod[2:3] * attn).astype(BF16)
        mixed[at_step(q)] = mix
        h_two[at_step(q, here.s * rows)] = norm_rows(mix.astype(F32), mod[3:4], mod[4:5]).astype(BF16)
        return carry

    lax.fori_loop(0, steps, norm_two, 0)
    gather_two = Gather(here, h_two, rows, [gather_sems.at[1, j] for j in range(4)])
    gather_two.start()
    scatter_two = Scatter(here, sums_two, rows, near_two, far_two, [scatter_sems.at[1, j] for j in range(4)])

    def feed_forward(block, i, other):
        at = rows_of(block, rows)
        hidden = jax.nn.gelu(dot(h_two[at], w_up[...]), approximate=True).astype(BF16)
        sums_two[at] = dot(hidden, w_down[...]).astype(BF16)
        if other:
            scatter_two.to_sibling(i).start()

    gather_two.each(feed_forward)
    for i in range(1, here.chips):
        scatter_two.pass_on(i)
    scatter_two.arrive()

    def step_mel(q, carry):
        feed = scatter_two.total((q * step, step))
        final = (mixed[at_step(q)].astype(F32) + mod[5:6] * feed).astype(BF16)
        normed = norm_rows(final.astype(F32), mod[6:7], mod[7:8]).astype(BF16)
        own = at_step(q, here.s * rows)
        mel_all[own] = noisy[own] + 0.5 * dot(normed, w_velocity[...])
        return carry

    lax.fori_loop(0, steps, step_mel, 0)
    gather_mel = Gather(here, mel_all, rows, [gather_sems.at[2, j] for j in range(4)])
    gather_mel.start()

    def hand_out(block, i, other):
        mel_out[rows_of(block, rows)] = mel_all[rows_of(block, rows)]

    gather_mel.each(hand_out)

    @pl.when(jnp.logical_not(last))
    def _():
        lookback(keys, 0).wait_send()
        lookback(values, 1).wait_send()

    for one in (gather, gather_two, gather_mel, scatter, scatter_two):
        one.finish()


def layer(frames, modulation, w_project, w_heads_out, w_up, w_down, w_velocity, noisy_mel):
    n = lax.axis_size("sub")
    rows, width = frames.shape
    total_rows = n * rows
    cols = w_project.shape[2]
    mel = noisy_mel.shape[1]
    chips = n // 2
    return pl.pallas_call(
        layer_kernel,
        out_shape=jax.ShapeDtypeStruct((total_rows, mel), F32),
        in_specs=[pl.BlockSpec(memory_space=VMEM)] * 8,
        out_specs=pl.BlockSpec(memory_space=VMEM),
        scratch_shapes=[
            VMEM((total_rows, width), BF16),
            VMEM((total_rows, width), BF16),
            VMEM((total_rows, cols), BF16),
            VMEM((total_rows + BLK, cols), BF16),
            VMEM((total_rows + BLK, cols), BF16),
            VMEM((BLK, cols), BF16),
            VMEM((total_rows, width), BF16),
            VMEM((total_rows, width), BF16),
            VMEM((chips, rows, width), BF16),
            VMEM((chips, rows, width), BF16),
            VMEM((chips, rows, width), BF16),
            VMEM((chips, rows, width), BF16),
            VMEM((rows, width), BF16),
            VMEM((total_rows, mel), F32),
            DMA((3, 4, chips)),
            DMA((2, 4, chips)),
            DMA((2,)),
            DMA((2,)),
        ],
        compiler_params=pltpu.CompilerParams(
            collective_id=0, has_side_effects=True, vmem_limit_bytes=48 * 2**20
        ),
        cost_estimate=pl.CostEstimate(flops=80 * 10**9, bytes_accessed=8 * 2**20, transcendentals=0),
        name="layer",
    )(frames, modulation, w_project, w_heads_out, w_up, w_down, w_velocity, noisy_mel)


def section_kernel(
    mel, w_prelude, w_upsample, alpha, w_dilated, w_plain, out,
    mel_wide, prelude, sums, near, far, up, taps, acts, woven, halo_low, halo_high,
    scatter_sems, edge_send, edge_recv,
):
    here = Place()
    total_rows, bands = mel.shape
    rows = total_rows // here.n
    mid = w_upsample.shape[2]
    s, t = here.s, here.t
    first, last = t == 0, t == here.times - 1
    begin, end = first & (s == 0), last & (s == here.n - 1)
    not_first, not_last = t > 0, t < here.times - 1
    behind, ahead = {"tm": t - 1}, {"tm": t + 1}
    spot = t * here.n + s
    low_spot, high_spot = spot - 1, spot + 1
    earlier = {"tm": low_spot // here.n, "sub": lax.rem(low_spot, here.n)}
    later = {"tm": high_spot // here.n, "sub": lax.rem(high_spot, here.n)}
    not_begin, not_end = spot > 0, spot < here.times * here.n - 1
    greet(here, ((not_first, behind), (not_last, ahead), (not_begin, earlier), (not_end, later)))

    zeros16 = jnp.zeros((16, bands), F32)

    mel_wide[pl.ds(0, 8)] = zeros16[:8]
    mel_wide[pl.ds(total_rows + 24, 8)] = zeros16[:8]

    @pl.when(first)
    def _():
        mel_wide[pl.ds(8, 8)] = zeros16[:8]

    @pl.when(last)
    def _():
        mel_wide[pl.ds(total_rows + 16, 8)] = zeros16[:8]

    mel_wide[pl.ds(16, total_rows)] = mel[...]
    mel_up = remote(
        mel_wide.at[pl.ds(total_rows + 8, 8)], mel_wide.at[pl.ds(8, 8)], edge_send.at[0], edge_recv.at[0], ahead
    )
    mel_down = remote(
        mel_wide.at[pl.ds(16, 8)], mel_wide.at[pl.ds(total_rows + 16, 8)], edge_send.at[1], edge_recv.at[1], behind
    )

    @pl.when(not_last)
    def _():
        mel_up.start()

    @pl.when(not_first)
    def _():
        mel_down.start()

    def prelude_rows(start, count):
        wide = mel_wide[pl.ds(start, count + 16)]
        total = jnp.zeros((count, w_prelude.shape[1]), F32)
        for j in range(w_prelude.shape[0]):
            total = total + dot_t(wide[5 + j : 5 + j + count].astype(BF16), w_prelude[j])
        return total.astype(BF16).astype(F32)

    @pl.when(not_first)
    def _():
        mel_up.wait_recv()

    @pl.when(not_last)
    def _():
        mel_down.wait_recv()

    def prelude_step(q, carry):
        base = pl.multiple_of(q * rows + 8, 8)
        prelude[pl.ds(base, rows)] = prelude_rows(base, rows)
        return carry

    lax.fori_loop(0, here.n, prelude_step, 0)
    prelude[pl.ds(0, 8)] = jnp.where(not_first, prelude_rows(0, 8), 0.0)
    prelude[pl.ds(total_rows + 8, 8)] = jnp.where(not_last, prelude_rows(total_rows + 8, 8), 0.0)

    scatter = Scatter(here, sums, rows, near, far, [scatter_sems.at[j] for j in range(4)])

    def upsample(block):
        wide = prelude[pl.ds(pl.multiple_of(block * rows, rows), rows + 16)]
        before = wide[7 : 7 + rows].astype(BF16)
        now = wide[8 : 8 + rows].astype(BF16)
        after = wide[9 : 9 + rows].astype(BF16)
        at = rows_of(block, rows)
        for phase in range(4):
            other, tap = (before, phase + 6) if phase < 2 else (after, phase - 2)
            result = dot(now, w_upsample[phase + 2]) + dot(other, w_upsample[tap])
            sums[at, phase * mid : (phase + 1) * mid] = result.astype(BF16)

    def upsample_step(p, carry):
        i = here.chips - 1 - p
        upsample(here.block(i, True))
        scatter.to_sibling(i).start()
        upsample(here.block(i, False))

        @pl.when(i > 0)
        def _():
            scatter.pass_on(i)

        return carry

    lax.fori_loop(0, here.chips, upsample_step, 0)
    scatter.arrive()

    step = min(64, rows)

    def total_step(q, carry):
        start = q * step
        up[pl.ds(pl.multiple_of(16 + start, 16), step)] = scatter.total((start, step)).astype(BF16)
        return carry

    lax.fori_loop(0, rows // step, total_step, 0)

    up_send = remote(up.at[pl.ds(rows, 16)], halo_low, edge_send.at[2], edge_recv.at[2], later)
    down_send = remote(up.at[pl.ds(16, 16)], halo_high, edge_send.at[3], edge_recv.at[3], earlier)

    @pl.when(not_end)
    def _():
        up_send.start()

    @pl.when(not_begin)
    def _():
        down_send.start()

    @pl.when(begin)
    def _():
        halo_low[...] = jnp.zeros(halo_low.shape, BF16)

    @pl.when(end)
    def _():
        halo_high[...] = jnp.zeros(halo_high.shape, BF16)

    alpha_one, alpha_two = alpha[0:1], alpha[1:2]

    def act_step(q, carry):
        start = q * step
        source = pl.ds(pl.multiple_of(16 + start, 16), step)
        target = pl.ds(pl.multiple_of(8 + start, 8), step)
        for phase in range(4):
            block = up[source, phase * mid : (phase + 1) * mid].astype(F32)
            acts[phase, target] = snake_act(block, alpha_one)
        return carry

    lax.fori_loop(0, rows // step, act_step, 0)

    @pl.when(not_begin)
    def _():
        up_send.wait_recv()

    @pl.when(not_end)
    def _():
        down_send.wait_recv()

    for phase in range(4):
        cols = slice(phase * mid, (phase + 1) * mid)
        acts[phase, pl.ds(0, 8)] = snake_act(halo_low[:, cols].astype(F32)[8:16], alpha_one)
        acts[phase, pl.ds(rows + 8, 8)] = snake_act(halo_high[:, cols].astype(F32)[0:8], alpha_one)

    length = rows + 16

    def prepare(befores, afters):
        for phase in range(4):
            block = acts[phase]
            taps[phase] = block.astype(BF16)
            if phase in befores:
                taps[4 + befores.index(phase)] = pltpu.roll(block, 1, 0).astype(BF16)
            if phase in afters:
                taps[4 + len(befores) + afters.index(phase)] = pltpu.roll(block, length - 1, 0).astype(BF16)

    chunk = 256 if mid % 256 == 0 else mid
    prepare((1, 2, 3), (0, 1, 2))
    line = lax.broadcasted_iota(jnp.int32, (length, 1), 0)
    outside = (begin & (line < 8)) | (end & (line >= rows + 8))
    row_mask = jnp.where(outside, 0.0, 1.0)

    def dilated_step(q, carry):
        cols = pl.ds(pl.multiple_of(q * chunk, chunk), chunk)
        row = alpha[1:2, cols]
        for phase in range(4):
            low = 4 + phase if phase < 3 else 0
            high = 3 if phase == 0 else 6 + phase
            inner = dot(taps[low], w_dilated[0, :, cols])
            inner = inner + dot(taps[phase], w_dilated[1, :, cols])
            inner = inner + dot(taps[high], w_dilated[2, :, cols])
            acts[phase, :, cols] = snake_act(inner, row) * row_mask
        return carry

    lax.fori_loop(0, mid // chunk, dilated_step, 0)
    prepare((3,), (0,))

    def plain_step(q, carry):
        cols = pl.ds(pl.multiple_of(q * chunk, chunk), chunk)
        for phase in range(4):
            low = 4 if phase == 0 else phase - 1
            high = 5 if phase == 3 else phase + 1
            outer = dot(taps[low], w_plain[0, :, cols])
            outer = outer + dot(taps[phase], w_plain[1, :, cols])
            outer = outer + dot(taps[high], w_plain[2, :, cols])
            base = up[pl.ds(16, rows), pl.ds(pl.multiple_of(phase * mid + q * chunk, chunk), chunk)]
            result = base.astype(F32) + outer[8 : 8 + rows]
            for lane in range(chunk // 128):
                woven[phase, :, pl.ds(pl.multiple_of(q * chunk + lane * 128, 128), 128)] = result[
                    :, lane * 128 : (lane + 1) * 128
                ]
        return carry

    lax.fori_loop(0, mid // chunk, plain_step, 0)

    def weave_step(q, carry):
        part = [woven[phase, pl.ds(pl.multiple_of(q * 16, 16), 16)] for phase in range(4)]
        out[pl.ds(pl.multiple_of(q * 64, 64), 64)] = jnp.stack(part, 1).reshape(64, mid).astype(BF16)
        return carry

    lax.fori_loop(0, rows // 16, weave_step, 0)

    @pl.when(not_last)
    def _():
        mel_up.wait_send()

    @pl.when(not_first)
    def _():
        mel_down.wait_send()

    @pl.when(not_end)
    def _():
        up_send.wait_send()

    @pl.when(not_begin)
    def _():
        down_send.wait_send()

    scatter.finish()


def section(mel, w_prelude, w_upsample, snake_alpha, w_dilated, w_plain):
    n = lax.axis_size("sub")
    chips = n // 2
    total_rows, bands = mel.shape
    rows = total_rows // n
    mid = w_upsample.shape[2]
    wide = 4 * mid
    return pl.pallas_call(
        section_kernel,
        out_shape=jax.ShapeDtypeStruct((4 * rows, mid), BF16),
        in_specs=[pl.BlockSpec(memory_space=VMEM)] * 6,
        out_specs=pl.BlockSpec(memory_space=VMEM),
        scratch_shapes=[
            VMEM((total_rows + 32, bands), F32),
            VMEM((total_rows + 16, w_prelude.shape[1]), F32),
            VMEM((total_rows, wide), BF16),
            VMEM((chips, rows, wide), BF16),
            VMEM((chips, rows, wide), BF16),
            VMEM((rows + 16, wide), BF16),
            VMEM((10, rows + 16, mid), BF16),
            VMEM((4, rows + 16, mid), F32),
            VMEM((4, rows, mid), F32),
            VMEM((16, wide), BF16),
            VMEM((16, wide), BF16),
            DMA((4, chips)),
            DMA((4,)),
            DMA((4,)),
        ],
        compiler_params=pltpu.CompilerParams(
            collective_id=1, has_side_effects=True, vmem_limit_bytes=58 * 2**20
        ),
        cost_estimate=pl.CostEstimate(flops=60 * 10**9, bytes_accessed=16 * 2**20, transcendentals=0),
        name="section",
    )(mel, w_prelude, w_upsample, snake_alpha, w_dilated, w_plain)


def body(
    frames, modulation, w_project, w_heads_out, w_up, w_down, w_velocity, noisy_mel, w_prelude,
    w_upsample, snake_alpha, w_dilated, w_plain,
):
    dilated_all = lax.all_gather(w_dilated, "sub", axis=1, tiled=True)
    plain_all = lax.all_gather(w_plain, "sub", axis=1, tiled=True)
    mel_next = layer(frames, modulation, w_project, w_heads_out, w_up, w_down, w_velocity, noisy_mel)
    section_out = section(mel_next, w_prelude, w_upsample, snake_alpha, dilated_all, plain_all)
    return (mel_next, section_out)


def solution(mesh):
    in_specs = (
        P(("tm", "sub"), None),
        P(),
        P(None, None, "sub"),
        P("sub", None),
        P(None, "sub"),
        P("sub", None),
        P(),
        P("tm", None),
        P(None, "sub", None),
        P(None, "sub", None),
        P(),
        P(None, "sub", None),
        P(None, "sub", None),
    )
    out_specs = (P("tm", None), P(("tm", "sub"), None))
    return jax.shard_map(body, mesh=mesh, in_specs=in_specs, out_specs=out_specs, check_vma=False)
```

```python
import functools
import math

import jax
import jax.numpy as jnp
from jax import lax
from jax.experimental import pallas as pl
from jax.experimental.pallas import tpu as pltpu
from jax.sharding import PartitionSpec as P

HEAD_DIM = 64
BLK = 256
EPSILON = 1e-06
MESH = pl.DeviceIdType.MESH
VMEM = pltpu.VMEM
DMA = pltpu.SemaphoreType.DMA
F32 = jnp.float32
BF16 = jnp.bfloat16


def norm_rows(rows, offset_row, scale_row):
    center = jnp.mean(rows, axis=-1, keepdims=True)
    square = jnp.mean(rows * rows, axis=-1, keepdims=True)
    spread = square - center * center
    return (rows - center) * lax.rsqrt(spread + EPSILON) * (1.0 + scale_row) + offset_row


def sin_squared(values):
    turns = jnp.round(values * (1.0 / math.pi))
    rest = values - turns * 3.140625
    rest = rest - turns * 9.670257568359375e-04
    rest = rest - turns * 6.2783295e-07
    rest = jnp.clip(rest, -0.5 * math.pi - 1e-3, 0.5 * math.pi + 1e-3)
    u = rest * rest
    series = -1.0 / 39916800.0
    for coefficient in (1.0 / 362880.0, -1.0 / 5040.0, 1.0 / 120.0, -1.0 / 6.0, 1.0):
        series = series * u + coefficient
    return u * series * series


def snake_act(values, alpha_row):
    return values + sin_squared(alpha_row * values) * (1.0 / alpha_row)


def dot(left, right):
    return jnp.dot(left, right, preferred_element_type=F32)


def dot_t(left, right):
    return lax.dot_general(left, right, (((1,), (1,)), ((), ())), preferred_element_type=F32)


class Place:
    def __init__(self):
        self.s = lax.axis_index("sub")
        self.t = lax.axis_index("tm")
        self.n = lax.axis_size("sub")
        self.times = lax.axis_size("tm")
        self.chips = self.n // 2
        self.core = lax.rem(self.s, 2)
        self.chip = self.s // 2
        self.sibling = self.s + 1 - 2 * self.core

    def chip_behind(self, i):
        return lax.rem(self.chip + self.chips - i, self.chips)

    def block(self, i, other_core):
        core = 1 - self.core if other_core else self.core
        return self.chip_behind(i) * 2 + core

    def peer(self, chip):
        return {"sub": chip * 2 + self.core}


def remote(src, dst, send, recv, device):
    return pltpu.make_async_remote_copy(
        src_ref=src, dst_ref=dst, send_sem=send, recv_sem=recv, device_id=device, device_id_type=MESH
    )


def rows_of(block, rows):
    return pl.ds(pl.multiple_of(block * rows, rows), rows)


class Gather:
    def __init__(self, here, buf, rows, sems):
        self.here, self.buf, self.rows = here, buf, rows
        self.x_send, self.x_recv, self.d_send, self.d_recv = sems

    def piece(self, block):
        return self.buf.at[rows_of(block, self.rows)]

    def across(self, i):
        here = self.here
        ahead = lax.rem(here.chip + i, here.chips)
        own = self.piece(here.s)
        return remote(own, own, self.x_send.at[i], self.x_recv.at[i], here.peer(ahead))

    def arriving(self, i):
        own = self.piece(self.here.block(i, False))
        return remote(own, own, self.x_send.at[i], self.x_recv.at[i], self.here.peer(self.here.chip_behind(i)))

    def forward(self, i):
        own = self.piece(self.here.block(i, False))
        return remote(own, own, self.d_send.at[i], self.d_recv.at[i], {"sub": self.here.sibling})

    def start(self):
        for i in range(1, self.here.chips):
            self.across(i).start()
        self.forward(0).start()

    def finish(self):
        for i in range(1, self.here.chips):
            self.across(i).wait_send()
        for i in range(self.here.chips):
            self.forward(i).wait_send()

    def each(self, work):
        here = self.here
        work(here.block(0, False), 0, False)
        self.take_other(0)
        work(here.block(0, True), 0, True)

        def step(i, carry):
            self.arriving(i).wait_recv()
            self.forward(i).start()
            work(here.block(i, False), i, False)
            self.take_other(i)
            work(here.block(i, True), i, True)
            return carry

        lax.fori_loop(1, here.chips, step, 0)

    def take_other(self, i):
        own = self.piece(self.here.block(i, True))
        remote(own, own, self.d_send.at[i], self.d_recv.at[i], {"sub": self.here.sibling}).wait_recv()


class WeightGather:
    def __init__(self, here, own, whole, sems):
        self.here, self.own, self.whole = here, own, whole
        self.x_send, self.x_recv, self.d_send, self.d_recv = sems

    def piece(self, block):
        return self.whole.at[:, rows_of(block, self.own.shape[1])]

    def local(self):
        return pltpu.make_async_copy(self.own, self.piece(self.here.s), self.x_send.at[0])

    def across(self, i):
        here = self.here
        ahead = lax.rem(here.chip + i, here.chips)
        return remote(self.own, self.piece(here.s), self.x_send.at[i], self.x_recv.at[i], here.peer(ahead))

    def forward(self, i):
        piece = self.piece(self.here.block(i, False))
        source = self.own if i == 0 else piece
        return remote(source, piece, self.d_send.at[i], self.d_recv.at[i], {"sub": self.here.sibling})

    def start(self):
        for i in range(1, self.here.chips):
            self.across(i).start()
        self.forward(0).start()
        self.local().start()

    def pass_on(self):
        for i in range(1, self.here.chips):
            self.across(i).wait_recv()
            self.forward(i).start()

    def finish(self):
        for i in range(self.here.chips):
            self.forward(i).wait()
        for i in range(1, self.here.chips):
            self.across(i).wait_send()
        self.local().wait()


class Scatter:
    def __init__(self, here, buf, rows, near, far, sems):
        self.here, self.buf, self.rows, self.near, self.far = here, buf, rows, near, far
        self.a_send, self.a_recv, self.b_send, self.b_recv = sems

    def piece(self, block):
        return self.buf.at[rows_of(block, self.rows)]

    def to_sibling(self, i):
        here = self.here
        return remote(
            self.piece(here.block(i, True)), self.near.at[i], self.a_send.at[i], self.a_recv.at[i],
            {"sub": here.sibling},
        )

    def to_chip(self, i):
        here = self.here
        return remote(
            self.piece(here.block(i, False)), self.far.at[i], self.b_send.at[i], self.b_recv.at[i],
            here.peer(here.chip_behind(i)),
        )

    def pass_on(self, i):
        self.to_sibling(i).wait_recv()
        here, rows = self.here, self.rows
        base = here.block(i, False) * rows
        step = min(64, rows)

        def add(q, carry):
            at = pl.ds(pl.multiple_of(base + q * step, step), step)
            near_at = pl.ds(pl.multiple_of(q * step, step), step)
            self.buf[at] = (self.buf[at].astype(F32) + self.near[i, near_at].astype(F32)).astype(BF16)
            return carry

        lax.fori_loop(0, rows // step, add, 0)
        self.to_chip(i).start()

    def arrive(self):
        self.to_sibling(0).wait_recv()
        for i in range(1, self.here.chips):
            self.to_chip(i).wait_recv()

    def total(self, at):
        start, size = at
        own = pl.ds(pl.multiple_of(self.here.s * self.rows + start, size), size)
        part = pl.ds(pl.multiple_of(start, size), size)
        total = self.buf[own].astype(F32) + self.near[0, part].astype(F32)
        for i in range(1, self.here.chips):
            total = total + self.far[i, part].astype(F32)
        return total

    def finish(self):
        for i in range(self.here.chips):
            self.to_sibling(i).wait_send()
        for i in range(1, self.here.chips):
            self.to_chip(i).wait_send()


def greet(here, extra=()):
    barrier = pltpu.get_barrier_semaphore()
    for i in range(1, here.chips):
        ahead = lax.rem(here.chip + i, here.chips)
        pl.semaphore_signal(barrier, inc=1, device_id=here.peer(ahead), device_id_type=MESH)
    pl.semaphore_signal(barrier, inc=1, device_id={"sub": here.sibling}, device_id_type=MESH)
    for condition, device in extra:

        @pl.when(condition)
        def _():
            pl.semaphore_signal(barrier, inc=1, device_id=device, device_id_type=MESH)

    greeted = here.chips
    for condition, device in extra:
        greeted = greeted + condition.astype(jnp.int32)
    pl.semaphore_wait(barrier, greeted)


def layer_kernel(
    frames, mod, w_project, w_heads_out, w_up, w_down, w_velocity, noisy, w_own, mel_out, w_all,
    h_one, h_two, queries, keys, values, attended, sums_one, sums_two, near_one, far_one, near_two,
    far_two, mixed, mel_all, gather_sems, scatter_sems, weight_sems, look_send, look_recv,
):
    here = Place()
    rows, width = frames.shape
    total_rows = here.n * rows
    step = min(64, rows)
    steps = rows // step
    first, last = here.t == 0, here.t == here.times - 1
    behind, ahead = {"tm": here.t - 1}, {"tm": here.t + 1}
    greet(here, ((here.t > 0, behind), (here.t < here.times - 1, ahead)))

    def at_step(q, base=0):
        return pl.ds(pl.multiple_of(base + q * step, step), step)

    def norm_one(q, carry):
        out = norm_rows(frames[at_step(q)].astype(F32), mod[0:1], mod[1:2])
        h_one[at_step(q, here.s * rows)] = out.astype(BF16)
        return carry

    lax.fori_loop(0, steps, norm_one, 0)
    gather = Gather(here, h_one, rows, [gather_sems.at[0, j] for j in range(4)])
    gather.start()

    def project(block, i, other):
        at = rows_of(block, rows)
        later = pl.ds(pl.multiple_of(BLK + block * rows, math.gcd(BLK, rows)), rows)
        h = h_one[at]
        queries[at] = (dot(h, w_project[0]).astype(BF16).astype(F32) * (1.0 / math.sqrt(HEAD_DIM))).astype(BF16)
        keys[later] = dot(h, w_project[1]).astype(BF16)
        values[later] = dot(h, w_project[2]).astype(BF16)

    gather.each(project)

    def lookback(buf, j):
        return remote(
            buf.at[pl.ds(total_rows, BLK)], buf.at[pl.ds(0, BLK)], look_send.at[j], look_recv.at[j], ahead
        )

    @pl.when(jnp.logical_not(last))
    def _():
        lookback(keys, 0).start()
        lookback(values, 1).start()

    weights = WeightGather(here, w_own, w_all, [weight_sems.at[j] for j in range(4)])
    weights.start()

    @pl.when(first)
    def _():
        keys[pl.ds(0, BLK)] = jnp.zeros((BLK, keys.shape[1]), BF16)
        values[pl.ds(0, BLK)] = jnp.zeros((BLK, values.shape[1]), BF16)

    blocks = total_rows // BLK
    heads = queries.shape[1] // HEAD_DIM

    scatter = Scatter(here, sums_one, rows, near_one, far_one, [scatter_sems.at[0, j] for j in range(4)])

    def attend(b):
        @pl.when(jnp.logical_and(b == 0, jnp.logical_not(first)))
        def _():
            lookback(keys, 0).wait_recv()
            lookback(values, 1).wait_recv()

        at = rows_of(b, BLK)
        both = pl.ds(pl.multiple_of(b * BLK, BLK), 2 * BLK)
        key_ids = lax.broadcasted_iota(jnp.int32, (1, 2 * BLK), 1)
        hidden_keys = jnp.where((key_ids < BLK) & (b == 0) & first, -1e30, 0.0)
        for head in range(heads):
            cols = slice(head * HEAD_DIM, (head + 1) * HEAD_DIM)
            scores = dot_t(queries[at, cols], keys[both, cols]) + hidden_keys
            raised = jnp.exp(scores - jnp.max(scores, axis=-1, keepdims=True))
            scale = 1.0 / jnp.sum(raised, axis=-1, keepdims=True)
            attended[:, cols] = (dot(raised.astype(BF16), values[both, cols]) * scale).astype(BF16)
        sums_one[at] = dot(attended[...], w_heads_out[...]).astype(BF16)

    if rows == BLK:
        def attend_step(p, carry):
            i = here.chips - 1 - p
            attend(here.block(i, True))
            scatter.to_sibling(i).start()
            attend(here.block(i, False))

            @pl.when(i > 0)
            def _():
                scatter.pass_on(i)

            return carry

        lax.fori_loop(0, here.chips, attend_step, 0)
    else:

        def attend_turn(turn, carry):
            attend(lax.rem(turn + 1, blocks))
            return carry

        lax.fori_loop(0, blocks, attend_turn, 0)
        for i in reversed(range(here.chips)):
            scatter.to_sibling(i).start()
        for i in range(1, here.chips):
            scatter.pass_on(i)
    scatter.arrive()

    def norm_two(q, carry):
        attn = scatter.total((q * step, step))
        mix = (frames[at_step(q)].astype(F32) + mod[2:3] * attn).astype(BF16)
        mixed[at_step(q)] = mix
        h_two[at_step(q, here.s * rows)] = norm_rows(mix.astype(F32), mod[3:4], mod[4:5]).astype(BF16)
        return carry

    lax.fori_loop(0, steps, norm_two, 0)
    gather_two = Gather(here, h_two, rows, [gather_sems.at[1, j] for j in range(4)])
    gather_two.start()
    weights.pass_on()
    scatter_two = Scatter(here, sums_two, rows, near_two, far_two, [scatter_sems.at[1, j] for j in range(4)])

    def feed_forward(block, i, other):
        at = rows_of(block, rows)
        hidden = jax.nn.gelu(dot(h_two[at], w_up[...]), approximate=True).astype(BF16)
        sums_two[at] = dot(hidden, w_down[...]).astype(BF16)
        if other:
            scatter_two.to_sibling(i).start()

    gather_two.each(feed_forward)
    for i in range(1, here.chips):
        scatter_two.pass_on(i)
    scatter_two.arrive()

    def step_mel(q, carry):
        feed = scatter_two.total((q * step, step))
        final = (mixed[at_step(q)].astype(F32) + mod[5:6] * feed).astype(BF16)
        normed = norm_rows(final.astype(F32), mod[6:7], mod[7:8]).astype(BF16)
        own = at_step(q, here.s * rows)
        mel_all[own] = noisy[own] + 0.5 * dot_t(normed, w_velocity[...])
        return carry

    lax.fori_loop(0, steps, step_mel, 0)
    gather_mel = Gather(here, mel_all, rows, [gather_sems.at[2, j] for j in range(4)])
    gather_mel.start()

    def hand_out(block, i, other):
        mel_out[rows_of(block, rows)] = mel_all[rows_of(block, rows)]

    gather_mel.each(hand_out)

    @pl.when(jnp.logical_not(last))
    def _():
        lookback(keys, 0).wait_send()
        lookback(values, 1).wait_send()

    for one in (gather, gather_two, gather_mel, scatter, scatter_two, weights):
        one.finish()


def layer(frames, modulation, w_project, w_heads_out, w_up, w_down, w_velocity, noisy_mel, w_own):
    n = lax.axis_size("sub")
    rows, width = frames.shape
    total_rows = n * rows
    cols = w_project.shape[2]
    mel = noisy_mel.shape[1]
    chips = n // 2
    return pl.pallas_call(
        layer_kernel,
        out_shape=(
            jax.ShapeDtypeStruct((total_rows, mel), F32),
            jax.ShapeDtypeStruct((w_own.shape[0], n * w_own.shape[1], w_own.shape[2]), BF16),
        ),
        in_specs=[pl.BlockSpec(memory_space=VMEM)] * 8 + [pl.BlockSpec(memory_space=pl.ANY)],
        out_specs=(pl.BlockSpec(memory_space=VMEM), pl.BlockSpec(memory_space=pl.ANY)),
        scratch_shapes=[
            VMEM((total_rows, width), BF16),
            VMEM((total_rows, width), BF16),
            VMEM((total_rows, cols), BF16),
            VMEM((total_rows + BLK, cols), BF16),
            VMEM((total_rows + BLK, cols), BF16),
            VMEM((BLK, cols), BF16),
            VMEM((total_rows, width), BF16),
            VMEM((total_rows, width), BF16),
            VMEM((chips, rows, width), BF16),
            VMEM((chips, rows, width), BF16),
            VMEM((chips, rows, width), BF16),
            VMEM((chips, rows, width), BF16),
            VMEM((rows, width), BF16),
            VMEM((total_rows, mel), F32),
            DMA((3, 4, chips)),
            DMA((2, 4, chips)),
            DMA((4, chips)),
            DMA((2,)),
            DMA((2,)),
        ],
        compiler_params=pltpu.CompilerParams(
            collective_id=0, has_side_effects=True, vmem_limit_bytes=48 * 2**20
        ),
        cost_estimate=pl.CostEstimate(flops=80 * 10**9, bytes_accessed=8 * 2**20, transcendentals=0),
        name="layer",
    )(frames, modulation, w_project, w_heads_out, w_up, w_down, w_velocity, noisy_mel, w_own)


def section_kernel(
    mel, w_prelude, w_upsample, alpha, w_dilated_all, w_plain_own, out,
    mel_wide, prelude, sums, near, far, up, taps, acts, woven, halo_low, halo_high,
    w_dilated, w_plain, scatter_sems, weight_sems, edge_send, edge_recv, load_sem,
):
    here = Place()
    total_rows, bands = mel.shape
    rows = total_rows // here.n
    mid = w_upsample.shape[2]
    s, t = here.s, here.t
    first, last = t == 0, t == here.times - 1
    begin, end = first & (s == 0), last & (s == here.n - 1)
    not_first, not_last = t > 0, t < here.times - 1
    behind, ahead = {"tm": t - 1}, {"tm": t + 1}
    spot = t * here.n + s
    low_spot, high_spot = spot - 1, spot + 1
    earlier = {"tm": low_spot // here.n, "sub": lax.rem(low_spot, here.n)}
    later = {"tm": high_spot // here.n, "sub": lax.rem(high_spot, here.n)}
    not_begin, not_end = spot > 0, spot < here.times * here.n - 1
    greet(here, ((not_first, behind), (not_last, ahead), (not_begin, earlier), (not_end, later)))

    load = pltpu.make_async_copy(w_dilated_all, w_dilated, load_sem)
    load.start()
    weights = WeightGather(here, w_plain_own, w_plain, [weight_sems.at[j] for j in range(4)])

    zeros16 = jnp.zeros((16, bands), F32)

    mel_wide[pl.ds(0, 8)] = zeros16[:8]
    mel_wide[pl.ds(total_rows + 24, 8)] = zeros16[:8]

    @pl.when(first)
    def _():
        mel_wide[pl.ds(8, 8)] = zeros16[:8]

    @pl.when(last)
    def _():
        mel_wide[pl.ds(total_rows + 16, 8)] = zeros16[:8]

    mel_wide[pl.ds(16, total_rows)] = mel[...]
    mel_up = remote(
        mel_wide.at[pl.ds(total_rows + 8, 8)], mel_wide.at[pl.ds(8, 8)], edge_send.at[0], edge_recv.at[0], ahead
    )
    mel_down = remote(
        mel_wide.at[pl.ds(16, 8)], mel_wide.at[pl.ds(total_rows + 16, 8)], edge_send.at[1], edge_recv.at[1], behind
    )

    @pl.when(not_last)
    def _():
        mel_up.start()

    @pl.when(not_first)
    def _():
        mel_down.start()

    def prelude_rows(start, count):
        wide = mel_wide[pl.ds(start, count + 16)]
        total = jnp.zeros((count, w_prelude.shape[2]), F32)
        for j in range(w_prelude.shape[0]):
            total = total + dot(wide[5 + j : 5 + j + count].astype(BF16), w_prelude[j])
        return total.astype(BF16).astype(F32)

    @pl.when(not_first)
    def _():
        mel_up.wait_recv()

    @pl.when(not_last)
    def _():
        mel_down.wait_recv()

    def prelude_step(q, carry):
        base = pl.multiple_of(q * rows + 8, 8)
        prelude[pl.ds(base, rows)] = prelude_rows(base, rows)
        return carry

    lax.fori_loop(0, here.n, prelude_step, 0)
    prelude[pl.ds(0, 8)] = jnp.where(not_first, prelude_rows(0, 8), 0.0)
    prelude[pl.ds(total_rows + 8, 8)] = jnp.where(not_last, prelude_rows(total_rows + 8, 8), 0.0)

    scatter = Scatter(here, sums, rows, near, far, [scatter_sems.at[j] for j in range(4)])

    def upsample(block):
        wide = prelude[pl.ds(pl.multiple_of(block * rows, rows), rows + 16)]
        before = wide[7 : 7 + rows].astype(BF16)
        now = wide[8 : 8 + rows].astype(BF16)
        after = wide[9 : 9 + rows].astype(BF16)
        at = rows_of(block, rows)
        for phase in range(4):
            other, tap = (before, phase + 6) if phase < 2 else (after, phase - 2)
            result = dot(now, w_upsample[phase + 2]) + dot(other, w_upsample[tap])
            sums[at, phase * mid : (phase + 1) * mid] = result.astype(BF16)

    def upsample_step(p, carry):
        i = here.chips - 1 - p
        upsample(here.block(i, True))
        scatter.to_sibling(i).start()
        upsample(here.block(i, False))

        @pl.when(i > 0)
        def _():
            scatter.pass_on(i)

        return carry

    lax.fori_loop(0, here.chips, upsample_step, 0)
    scatter.arrive()

    step = min(64, rows)

    def total_step(q, carry):
        start = q * step
        up[pl.ds(pl.multiple_of(16 + start, 16), step)] = scatter.total((start, step)).astype(BF16)
        return carry

    lax.fori_loop(0, rows // step, total_step, 0)

    up_send = remote(up.at[pl.ds(rows, 16)], halo_low, edge_send.at[2], edge_recv.at[2], later)
    down_send = remote(up.at[pl.ds(16, 16)], halo_high, edge_send.at[3], edge_recv.at[3], earlier)

    @pl.when(not_end)
    def _():
        up_send.start()

    @pl.when(not_begin)
    def _():
        down_send.start()

    weights.start()

    @pl.when(begin)
    def _():
        halo_low[...] = jnp.zeros(halo_low.shape, BF16)

    @pl.when(end)
    def _():
        halo_high[...] = jnp.zeros(halo_high.shape, BF16)

    alpha_one, alpha_two = alpha[0:1], alpha[1:2]

    def act_step(q, carry):
        start = q * step
        source = pl.ds(pl.multiple_of(16 + start, 16), step)
        target = pl.ds(pl.multiple_of(8 + start, 8), step)
        for phase in range(4):
            block = up[source, phase * mid : (phase + 1) * mid].astype(F32)
            acts[phase, target] = snake_act(block, alpha_one)
        return carry

    lax.fori_loop(0, rows // step, act_step, 0)

    @pl.when(not_begin)
    def _():
        up_send.wait_recv()

    @pl.when(not_end)
    def _():
        down_send.wait_recv()

    for phase in range(4):
        cols = slice(phase * mid, (phase + 1) * mid)
        acts[phase, pl.ds(0, 8)] = snake_act(halo_low[:, cols].astype(F32)[8:16], alpha_one)
        acts[phase, pl.ds(rows + 8, 8)] = snake_act(halo_high[:, cols].astype(F32)[0:8], alpha_one)

    length = rows + 16

    def prepare(befores, afters):
        for phase in range(4):
            block = acts[phase]
            taps[phase] = block.astype(BF16)
            if phase in befores:
                taps[4 + befores.index(phase)] = pltpu.roll(block, 1, 0).astype(BF16)
            if phase in afters:
                taps[4 + len(befores) + afters.index(phase)] = pltpu.roll(block, length - 1, 0).astype(BF16)

    chunk = 256 if mid % 256 == 0 else mid
    prepare((1, 2, 3), (0, 1, 2))
    line = lax.broadcasted_iota(jnp.int32, (length, 1), 0)
    outside = (begin & (line < 8)) | (end & (line >= rows + 8))
    row_mask = jnp.where(outside, 0.0, 1.0)

    load.wait()

    def dilated_step(q, carry):
        cols = pl.ds(pl.multiple_of(q * chunk, chunk), chunk)
        row = alpha[1:2, cols]
        for phase in range(4):
            low = 4 + phase if phase < 3 else 0
            high = 3 if phase == 0 else 6 + phase
            inner = dot(taps[low], w_dilated[0, :, cols])
            inner = inner + dot(taps[phase], w_dilated[1, :, cols])
            inner = inner + dot(taps[high], w_dilated[2, :, cols])
            acts[phase, :, cols] = snake_act(inner, row) * row_mask
        return carry

    lax.fori_loop(0, mid // chunk, dilated_step, 0)
    weights.pass_on()
    prepare((3,), (0,))
    weights.finish()

    def plain_step(q, carry):
        cols = pl.ds(pl.multiple_of(q * chunk, chunk), chunk)
        for phase in range(4):
            low = 4 if phase == 0 else phase - 1
            high = 5 if phase == 3 else phase + 1
            outer = dot(taps[low], w_plain[0, :, cols])
            outer = outer + dot(taps[phase], w_plain[1, :, cols])
            outer = outer + dot(taps[high], w_plain[2, :, cols])
            base = up[pl.ds(16, rows), pl.ds(pl.multiple_of(phase * mid + q * chunk, chunk), chunk)]
            result = base.astype(F32) + outer[8 : 8 + rows]
            for lane in range(chunk // 128):
                woven[phase, :, pl.ds(pl.multiple_of(q * chunk + lane * 128, 128), 128)] = result[
                    :, lane * 128 : (lane + 1) * 128
                ]
        return carry

    lax.fori_loop(0, mid // chunk, plain_step, 0)

    def weave_step(q, carry):
        part = [woven[phase, pl.ds(pl.multiple_of(q * 16, 16), 16)] for phase in range(4)]
        out[pl.ds(pl.multiple_of(q * 64, 64), 64)] = jnp.stack(part, 1).reshape(64, mid).astype(BF16)
        return carry

    lax.fori_loop(0, rows // 16, weave_step, 0)

    @pl.when(not_last)
    def _():
        mel_up.wait_send()

    @pl.when(not_first)
    def _():
        mel_down.wait_send()

    @pl.when(not_end)
    def _():
        up_send.wait_send()

    @pl.when(not_begin)
    def _():
        down_send.wait_send()

    scatter.finish()


def section(mel, w_prelude, w_upsample, snake_alpha, w_dilated, w_plain):
    n = lax.axis_size("sub")
    chips = n // 2
    total_rows, bands = mel.shape
    rows = total_rows // n
    mid = w_upsample.shape[2]
    wide = 4 * mid
    return pl.pallas_call(
        section_kernel,
        out_shape=jax.ShapeDtypeStruct((4 * rows, mid), BF16),
        in_specs=[pl.BlockSpec(memory_space=VMEM)] * 4 + [pl.BlockSpec(memory_space=pl.ANY)] * 2,
        out_specs=pl.BlockSpec(memory_space=VMEM),
        scratch_shapes=[
            VMEM((total_rows + 32, bands), F32),
            VMEM((total_rows + 16, w_prelude.shape[2]), F32),
            VMEM((total_rows, wide), BF16),
            VMEM((chips, rows, wide), BF16),
            VMEM((chips, rows, wide), BF16),
            VMEM((rows + 16, wide), BF16),
            VMEM((10, rows + 16, mid), BF16),
            VMEM((4, rows + 16, mid), F32),
            VMEM((4, rows, mid), F32),
            VMEM((16, wide), BF16),
            VMEM((16, wide), BF16),
            VMEM(w_dilated.shape, BF16),
            VMEM(w_dilated.shape, BF16),
            DMA((4, chips)),
            DMA((4, chips)),
            DMA((4,)),
            DMA((4,)),
            DMA,
        ],
        compiler_params=pltpu.CompilerParams(
            collective_id=1, has_side_effects=True, vmem_limit_bytes=58 * 2**20
        ),
        cost_estimate=pl.CostEstimate(flops=60 * 10**9, bytes_accessed=16 * 2**20, transcendentals=0),
        name="section",
    )(mel, w_prelude, w_upsample, snake_alpha, w_dilated, w_plain)


def body(
    frames, modulation, w_project, w_heads_out, w_up, w_down, w_velocity, noisy_mel, w_prelude,
    w_upsample, snake_alpha, w_dilated, w_plain,
):
    mel_next, dilated_all = layer(
        frames, modulation, w_project, w_heads_out, w_up, w_down, w_velocity.T, noisy_mel, w_dilated
    )
    section_out = section(
        mel_next, jnp.swapaxes(w_prelude, 1, 2), w_upsample, snake_alpha, dilated_all, w_plain
    )
    return (mel_next, section_out)


def solution(mesh):
    in_specs = (
        P(("tm", "sub"), None),
        P(),
        P(None, None, "sub"),
        P("sub", None),
        P(None, "sub"),
        P("sub", None),
        P(),
        P("tm", None),
        P(None, "sub", None),
        P(None, "sub", None),
        P(),
        P(None, "sub", None),
        P(None, "sub", None),
    )
    out_specs = (P("tm", None), P(("tm", "sub"), None))
    return jax.shard_map(body, mesh=mesh, in_specs=in_specs, out_specs=out_specs, check_vma=False)
```

```python
import functools
import math

import jax
import jax.numpy as jnp
from jax import lax
from jax.experimental import pallas as pl
from jax.experimental.pallas import tpu as pltpu
from jax.sharding import PartitionSpec as P

HEAD_DIM = 64
BLK = 256
EPSILON = 1e-06
MESH = pl.DeviceIdType.MESH
VMEM = pltpu.VMEM
DMA = pltpu.SemaphoreType.DMA
F32 = jnp.float32
BF16 = jnp.bfloat16


def norm_rows(rows, offset_row, scale_row):
    center = jnp.mean(rows, axis=-1, keepdims=True)
    square = jnp.mean(rows * rows, axis=-1, keepdims=True)
    spread = square - center * center
    return (rows - center) * lax.rsqrt(spread + EPSILON) * (1.0 + scale_row) + offset_row


def sin_squared(values):
    turns = jnp.round(values * (1.0 / math.pi))
    rest = values - turns * 3.140625
    rest = rest - turns * 9.670257568359375e-04
    rest = rest - turns * 6.2783295e-07
    rest = jnp.clip(rest, -0.5 * math.pi - 1e-3, 0.5 * math.pi + 1e-3)
    u = rest * rest
    series = -1.0 / 39916800.0
    for coefficient in (1.0 / 362880.0, -1.0 / 5040.0, 1.0 / 120.0, -1.0 / 6.0, 1.0):
        series = series * u + coefficient
    return u * series * series


def snake_act(values, alpha_row):
    return values + sin_squared(alpha_row * values) * (1.0 / alpha_row)


def dot(left, right):
    return jnp.dot(left, right, preferred_element_type=F32)


def dot_t(left, right):
    return lax.dot_general(left, right, (((1,), (1,)), ((), ())), preferred_element_type=F32)


class Place:
    def __init__(self):
        self.s = lax.axis_index("sub")
        self.t = lax.axis_index("tm")
        self.n = lax.axis_size("sub")
        self.times = lax.axis_size("tm")
        self.chips = self.n // 2
        self.core = lax.rem(self.s, 2)
        self.chip = self.s // 2
        self.sibling = self.s + 1 - 2 * self.core

    def chip_behind(self, i):
        return lax.rem(self.chip + self.chips - i, self.chips)

    def block(self, i, other_core):
        core = 1 - self.core if other_core else self.core
        return self.chip_behind(i) * 2 + core

    def peer(self, chip):
        return {"sub": chip * 2 + self.core}


def remote(src, dst, send, recv, device):
    return pltpu.make_async_remote_copy(
        src_ref=src, dst_ref=dst, send_sem=send, recv_sem=recv, device_id=device, device_id_type=MESH
    )


def rows_of(block, rows):
    return pl.ds(pl.multiple_of(block * rows, rows), rows)


class Gather:
    def __init__(self, here, buf, rows, sems):
        self.here, self.buf, self.rows = here, buf, rows
        self.x_send, self.x_recv, self.d_send, self.d_recv = sems

    def piece(self, block):
        return self.buf.at[rows_of(block, self.rows)]

    def across(self, i):
        here = self.here
        ahead = lax.rem(here.chip + i, here.chips)
        own = self.piece(here.s)
        return remote(own, own, self.x_send.at[i], self.x_recv.at[i], here.peer(ahead))

    def arriving(self, i):
        own = self.piece(self.here.block(i, False))
        return remote(own, own, self.x_send.at[i], self.x_recv.at[i], self.here.peer(self.here.chip_behind(i)))

    def forward(self, i):
        own = self.piece(self.here.block(i, False))
        return remote(own, own, self.d_send.at[i], self.d_recv.at[i], {"sub": self.here.sibling})

    def start(self):
        for i in range(1, self.here.chips):
            self.across(i).start()
        self.forward(0).start()

    def finish(self):
        for i in range(1, self.here.chips):
            self.across(i).wait_send()
        for i in range(self.here.chips):
            self.forward(i).wait_send()

    def each(self, work):
        here = self.here
        work(here.block(0, False), 0, False)
        self.take_other(0)
        work(here.block(0, True), 0, True)

        def step(i, carry):
            self.arriving(i).wait_recv()
            self.forward(i).start()
            work(here.block(i, False), i, False)
            self.take_other(i)
            work(here.block(i, True), i, True)
            return carry

        lax.fori_loop(1, here.chips, step, 0)

    def take_other(self, i):
        own = self.piece(self.here.block(i, True))
        remote(own, own, self.d_send.at[i], self.d_recv.at[i], {"sub": self.here.sibling}).wait_recv()


class WeightGather:
    def __init__(self, here, own, whole, sems):
        self.here, self.own, self.whole = here, own, whole
        self.x_send, self.x_recv, self.d_send, self.d_recv, self.t_send, self.t_recv = sems
        half = own.shape[2] // 2
        odd = lax.rem(here.t, 2)
        self.cols = pl.ds(pl.multiple_of(odd * half, half), half)
        self.partner = {"tm": here.t + 1 - 2 * odd}

    def rows(self, block):
        return rows_of(block, self.own.shape[1])

    def piece(self, block):
        return self.whole.at[:, self.rows(block)]

    def local(self):
        return pltpu.make_async_copy(self.own, self.piece(self.here.s), self.x_send.at[0])

    def across(self, i):
        here = self.here
        ahead = lax.rem(here.chip + i, here.chips)
        source = self.own.at[:, :, self.cols]
        target = self.whole.at[:, self.rows(here.s), self.cols]
        return remote(source, target, self.x_send.at[i], self.x_recv.at[i], here.peer(ahead))

    def along(self, i):
        half = self.whole.at[:, self.rows(self.here.block(i, False)), self.cols]
        return remote(half, half, self.t_send.at[i], self.t_recv.at[i], self.partner)

    def forward(self, i):
        piece = self.piece(self.here.block(i, False))
        source = self.own if i == 0 else piece
        return remote(source, piece, self.d_send.at[i], self.d_recv.at[i], {"sub": self.here.sibling})

    def start(self):
        for i in range(1, self.here.chips):
            self.across(i).start()
        self.forward(0).start()
        self.local().start()

    def exchange(self):
        for i in range(1, self.here.chips):
            self.across(i).wait_recv()
            self.along(i).start()

    def pass_on(self):
        for i in range(1, self.here.chips):
            self.along(i).wait_recv()
            self.forward(i).start()

    def finish(self):
        for i in range(self.here.chips):
            self.forward(i).wait()
        for i in range(1, self.here.chips):
            self.across(i).wait_send()
            self.along(i).wait_send()
        self.local().wait()


class Scatter:
    def __init__(self, here, buf, rows, near, far, sems):
        self.here, self.buf, self.rows, self.near, self.far = here, buf, rows, near, far
        self.a_send, self.a_recv, self.b_send, self.b_recv = sems

    def piece(self, block):
        return self.buf.at[rows_of(block, self.rows)]

    def to_sibling(self, i):
        here = self.here
        return remote(
            self.piece(here.block(i, True)), self.near.at[i], self.a_send.at[i], self.a_recv.at[i],
            {"sub": here.sibling},
        )

    def to_chip(self, i):
        here = self.here
        return remote(
            self.piece(here.block(i, False)), self.far.at[i], self.b_send.at[i], self.b_recv.at[i],
            here.peer(here.chip_behind(i)),
        )

    def pass_on(self, i):
        self.to_sibling(i).wait_recv()
        here, rows = self.here, self.rows
        base = here.block(i, False) * rows
        step = min(64, rows)

        def add(q, carry):
            at = pl.ds(pl.multiple_of(base + q * step, step), step)
            near_at = pl.ds(pl.multiple_of(q * step, step), step)
            self.buf[at] = (self.buf[at].astype(F32) + self.near[i, near_at].astype(F32)).astype(BF16)
            return carry

        lax.fori_loop(0, rows // step, add, 0)
        self.to_chip(i).start()

    def arrive(self):
        self.to_sibling(0).wait_recv()
        for i in range(1, self.here.chips):
            self.to_chip(i).wait_recv()

    def total(self, at):
        start, size = at
        own = pl.ds(pl.multiple_of(self.here.s * self.rows + start, size), size)
        part = pl.ds(pl.multiple_of(start, size), size)
        total = self.buf[own].astype(F32) + self.near[0, part].astype(F32)
        for i in range(1, self.here.chips):
            total = total + self.far[i, part].astype(F32)
        return total

    def finish(self):
        for i in range(self.here.chips):
            self.to_sibling(i).wait_send()
        for i in range(1, self.here.chips):
            self.to_chip(i).wait_send()


def greet(here, extra=()):
    barrier = pltpu.get_barrier_semaphore()
    for i in range(1, here.chips):
        ahead = lax.rem(here.chip + i, here.chips)
        pl.semaphore_signal(barrier, inc=1, device_id=here.peer(ahead), device_id_type=MESH)
    pl.semaphore_signal(barrier, inc=1, device_id={"sub": here.sibling}, device_id_type=MESH)
    for condition, device in extra:

        @pl.when(condition)
        def _():
            pl.semaphore_signal(barrier, inc=1, device_id=device, device_id_type=MESH)

    greeted = here.chips
    for condition, device in extra:
        greeted = greeted + condition.astype(jnp.int32)
    pl.semaphore_wait(barrier, greeted)


def layer_kernel(
    frames, mod, project_in, heads_out_in, up_in, down_in, w_velocity, noisy, w_own, mel_out, w_all,
    h_one, h_two, queries, keys, values, attended, sums_one, sums_two, near_one, far_one, near_two,
    far_two, mixed, mel_all, gather_sems, scatter_sems, weight_sems, load_sems, w_project, w_heads_out, w_up, w_down,
    look_send, look_recv,
):
    here = Place()
    rows, width = frames.shape
    total_rows = here.n * rows
    step = min(64, rows)
    steps = rows // step
    first, last = here.t == 0, here.t == here.times - 1
    behind, ahead = {"tm": here.t - 1}, {"tm": here.t + 1}
    held = ((project_in, w_project), (heads_out_in, w_heads_out), (up_in, w_up), (down_in, w_down))
    loads = [pltpu.make_async_copy(*pair, load_sems.at[j]) for j, pair in enumerate(held)]
    for load in loads:
        load.start()
    greet(here, ((here.t > 0, behind), (here.t < here.times - 1, ahead)))

    def at_step(q, base=0):
        return pl.ds(pl.multiple_of(base + q * step, step), step)

    def norm_one(q, carry):
        out = norm_rows(frames[at_step(q)].astype(F32), mod[0:1], mod[1:2])
        h_one[at_step(q, here.s * rows)] = out.astype(BF16)
        return carry

    lax.fori_loop(0, steps, norm_one, 0)
    gather = Gather(here, h_one, rows, [gather_sems.at[0, j] for j in range(4)])
    gather.start()

    def project(block, i, other):
        at = rows_of(block, rows)
        later = pl.ds(pl.multiple_of(BLK + block * rows, math.gcd(BLK, rows)), rows)
        h = h_one[at]
        queries[at] = (dot(h, w_project[0]).astype(BF16).astype(F32) * (1.0 / math.sqrt(HEAD_DIM))).astype(BF16)
        keys[later] = dot(h, w_project[1]).astype(BF16)
        values[later] = dot(h, w_project[2]).astype(BF16)

    loads[0].wait()
    gather.each(project)

    def lookback(buf, j):
        return remote(
            buf.at[pl.ds(total_rows, BLK)], buf.at[pl.ds(0, BLK)], look_send.at[j], look_recv.at[j], ahead
        )

    @pl.when(jnp.logical_not(last))
    def _():
        lookback(keys, 0).start()
        lookback(values, 1).start()

    weights = WeightGather(here, w_own, w_all, [weight_sems.at[j] for j in range(6)])
    weights.start()

    @pl.when(first)
    def _():
        keys[pl.ds(0, BLK)] = jnp.zeros((BLK, keys.shape[1]), BF16)
        values[pl.ds(0, BLK)] = jnp.zeros((BLK, values.shape[1]), BF16)

    blocks = total_rows // BLK
    heads = queries.shape[1] // HEAD_DIM

    scatter = Scatter(here, sums_one, rows, near_one, far_one, [scatter_sems.at[0, j] for j in range(4)])

    loads[1].wait()

    def attend(b):
        @pl.when(jnp.logical_and(b == 0, jnp.logical_not(first)))
        def _():
            lookback(keys, 0).wait_recv()
            lookback(values, 1).wait_recv()

        at = rows_of(b, BLK)
        both = pl.ds(pl.multiple_of(b * BLK, BLK), 2 * BLK)
        key_ids = lax.broadcasted_iota(jnp.int32, (1, 2 * BLK), 1)
        hidden_keys = jnp.where((key_ids < BLK) & (b == 0) & first, -1e30, 0.0)
        for head in range(heads):
            cols = slice(head * HEAD_DIM, (head + 1) * HEAD_DIM)
            scores = dot_t(queries[at, cols], keys[both, cols]) + hidden_keys
            raised = jnp.exp(scores - jnp.max(scores, axis=-1, keepdims=True))
            scale = 1.0 / jnp.sum(raised, axis=-1, keepdims=True)
            attended[:, cols] = (dot(raised.astype(BF16), values[both, cols]) * scale).astype(BF16)
        sums_one[at] = dot(attended[...], w_heads_out[...]).astype(BF16)

    if rows == BLK:
        def attend_step(p, carry):
            i = here.chips - 1 - p
            attend(here.block(i, True))
            scatter.to_sibling(i).start()
            attend(here.block(i, False))

            @pl.when(i > 0)
            def _():
                scatter.pass_on(i)

            return carry

        lax.fori_loop(0, here.chips, attend_step, 0)
    else:

        def attend_turn(turn, carry):
            attend(lax.rem(turn + 1, blocks))
            return carry

        lax.fori_loop(0, blocks, attend_turn, 0)
        for i in reversed(range(here.chips)):
            scatter.to_sibling(i).start()
        for i in range(1, here.chips):
            scatter.pass_on(i)
    weights.exchange()
    scatter.arrive()

    def norm_two(q, carry):
        attn = scatter.total((q * step, step))
        mix = (frames[at_step(q)].astype(F32) + mod[2:3] * attn).astype(BF16)
        mixed[at_step(q)] = mix
        h_two[at_step(q, here.s * rows)] = norm_rows(mix.astype(F32), mod[3:4], mod[4:5]).astype(BF16)
        return carry

    lax.fori_loop(0, steps, norm_two, 0)
    gather_two = Gather(here, h_two, rows, [gather_sems.at[1, j] for j in range(4)])
    gather_two.start()
    weights.pass_on()
    scatter_two = Scatter(here, sums_two, rows, near_two, far_two, [scatter_sems.at[1, j] for j in range(4)])

    def feed_forward(block, i, other):
        at = rows_of(block, rows)
        hidden = jax.nn.gelu(dot(h_two[at], w_up[...]), approximate=True).astype(BF16)
        sums_two[at] = dot(hidden, w_down[...]).astype(BF16)
        if other:
            scatter_two.to_sibling(i).start()

    loads[2].wait()
    loads[3].wait()
    gather_two.each(feed_forward)
    for i in range(1, here.chips):
        scatter_two.pass_on(i)
    scatter_two.arrive()

    def step_mel(q, carry):
        feed = scatter_two.total((q * step, step))
        final = (mixed[at_step(q)].astype(F32) + mod[5:6] * feed).astype(BF16)
        normed = norm_rows(final.astype(F32), mod[6:7], mod[7:8]).astype(BF16)
        own = at_step(q, here.s * rows)
        mel_all[own] = noisy[own] + 0.5 * dot_t(normed, w_velocity[...])
        return carry

    lax.fori_loop(0, steps, step_mel, 0)
    gather_mel = Gather(here, mel_all, rows, [gather_sems.at[2, j] for j in range(4)])
    gather_mel.start()

    def hand_out(block, i, other):
        mel_out[rows_of(block, rows)] = mel_all[rows_of(block, rows)]

    gather_mel.each(hand_out)

    @pl.when(jnp.logical_not(last))
    def _():
        lookback(keys, 0).wait_send()
        lookback(values, 1).wait_send()

    for one in (gather, gather_two, gather_mel, scatter, scatter_two, weights):
        one.finish()


def layer(frames, modulation, w_project, w_heads_out, w_up, w_down, w_velocity, noisy_mel, w_own):
    n = lax.axis_size("sub")
    rows, width = frames.shape
    total_rows = n * rows
    cols = w_project.shape[2]
    mel = noisy_mel.shape[1]
    chips = n // 2
    return pl.pallas_call(
        layer_kernel,
        out_shape=(
            jax.ShapeDtypeStruct((total_rows, mel), F32),
            jax.ShapeDtypeStruct((w_own.shape[0], n * w_own.shape[1], w_own.shape[2]), BF16),
        ),
        in_specs=[
            pl.BlockSpec(memory_space=space)
            for space in [VMEM] * 2 + [pl.ANY] * 4 + [VMEM] * 2 + [pl.ANY]
        ],
        out_specs=(pl.BlockSpec(memory_space=VMEM), pl.BlockSpec(memory_space=pl.ANY)),
        scratch_shapes=[
            VMEM((total_rows, width), BF16),
            VMEM((total_rows, width), BF16),
            VMEM((total_rows, cols), BF16),
            VMEM((total_rows + BLK, cols), BF16),
            VMEM((total_rows + BLK, cols), BF16),
            VMEM((BLK, cols), BF16),
            VMEM((total_rows, width), BF16),
            VMEM((total_rows, width), BF16),
            VMEM((chips, rows, width), BF16),
            VMEM((chips, rows, width), BF16),
            VMEM((chips, rows, width), BF16),
            VMEM((chips, rows, width), BF16),
            VMEM((rows, width), BF16),
            VMEM((total_rows, mel), F32),
            DMA((3, 4, chips)),
            DMA((2, 4, chips)),
            DMA((6, chips)),
            DMA((4,)),
            VMEM(w_project.shape, BF16),
            VMEM(w_heads_out.shape, BF16),
            VMEM(w_up.shape, BF16),
            VMEM(w_down.shape, BF16),
            DMA((2,)),
            DMA((2,)),
        ],
        compiler_params=pltpu.CompilerParams(
            collective_id=0, has_side_effects=True, vmem_limit_bytes=60 * 2**20
        ),
        cost_estimate=pl.CostEstimate(flops=80 * 10**9, bytes_accessed=8 * 2**20, transcendentals=0),
        name="layer",
    )(frames, modulation, w_project, w_heads_out, w_up, w_down, w_velocity, noisy_mel, w_own)


def section_kernel(
    mel, w_prelude, w_upsample_in, alpha, w_dilated_all, w_plain_own, out,
    mel_wide, prelude, sums, near, far, up, taps, acts, woven, halo_low, halo_high,
    w_dilated, w_plain, w_upsample, scatter_sems, weight_sems, edge_send, edge_recv, load_sems,
):
    here = Place()
    total_rows, bands = mel.shape
    rows = total_rows // here.n
    mid = w_upsample.shape[2]
    s, t = here.s, here.t
    first, last = t == 0, t == here.times - 1
    begin, end = first & (s == 0), last & (s == here.n - 1)
    not_first, not_last = t > 0, t < here.times - 1
    behind, ahead = {"tm": t - 1}, {"tm": t + 1}
    spot = t * here.n + s
    low_spot, high_spot = spot - 1, spot + 1
    earlier = {"tm": low_spot // here.n, "sub": lax.rem(low_spot, here.n)}
    later = {"tm": high_spot // here.n, "sub": lax.rem(high_spot, here.n)}
    not_begin, not_end = spot > 0, spot < here.times * here.n - 1
    load_up = pltpu.make_async_copy(w_upsample_in, w_upsample, load_sems.at[0])
    load_up.start()
    load = pltpu.make_async_copy(w_dilated_all, w_dilated, load_sems.at[1])
    load.start()
    greet(here, ((not_first, behind), (not_last, ahead), (not_begin, earlier), (not_end, later)))

    weights = WeightGather(here, w_plain_own, w_plain, [weight_sems.at[j] for j in range(6)])

    zeros16 = jnp.zeros((16, bands), F32)

    mel_wide[pl.ds(0, 8)] = zeros16[:8]
    mel_wide[pl.ds(total_rows + 24, 8)] = zeros16[:8]

    @pl.when(first)
    def _():
        mel_wide[pl.ds(8, 8)] = zeros16[:8]

    @pl.when(last)
    def _():
        mel_wide[pl.ds(total_rows + 16, 8)] = zeros16[:8]

    mel_wide[pl.ds(16, total_rows)] = mel[...]
    mel_up = remote(
        mel_wide.at[pl.ds(total_rows + 8, 8)], mel_wide.at[pl.ds(8, 8)], edge_send.at[0], edge_recv.at[0], ahead
    )
    mel_down = remote(
        mel_wide.at[pl.ds(16, 8)], mel_wide.at[pl.ds(total_rows + 16, 8)], edge_send.at[1], edge_recv.at[1], behind
    )

    @pl.when(not_last)
    def _():
        mel_up.start()

    @pl.when(not_first)
    def _():
        mel_down.start()

    weights.start()

    def prelude_rows(start, count):
        wide = mel_wide[pl.ds(start, count + 16)]
        total = jnp.zeros((count, w_prelude.shape[2]), F32)
        for j in range(w_prelude.shape[0]):
            total = total + dot(wide[5 + j : 5 + j + count].astype(BF16), w_prelude[j])
        return total.astype(BF16).astype(F32)

    @pl.when(not_first)
    def _():
        mel_up.wait_recv()

    @pl.when(not_last)
    def _():
        mel_down.wait_recv()

    def prelude_step(q, carry):
        base = pl.multiple_of(q * rows + 8, 8)
        prelude[pl.ds(base, rows)] = prelude_rows(base, rows)
        return carry

    lax.fori_loop(0, here.n, prelude_step, 0)
    prelude[pl.ds(0, 8)] = jnp.where(not_first, prelude_rows(0, 8), 0.0)
    prelude[pl.ds(total_rows + 8, 8)] = jnp.where(not_last, prelude_rows(total_rows + 8, 8), 0.0)

    scatter = Scatter(here, sums, rows, near, far, [scatter_sems.at[j] for j in range(4)])

    def upsample(block):
        wide = prelude[pl.ds(pl.multiple_of(block * rows, rows), rows + 16)]
        before = wide[7 : 7 + rows].astype(BF16)
        now = wide[8 : 8 + rows].astype(BF16)
        after = wide[9 : 9 + rows].astype(BF16)
        at = rows_of(block, rows)
        for phase in range(4):
            other, tap = (before, phase + 6) if phase < 2 else (after, phase - 2)
            result = dot(now, w_upsample[phase + 2]) + dot(other, w_upsample[tap])
            sums[at, phase * mid : (phase + 1) * mid] = result.astype(BF16)

    def upsample_step(p, carry):
        i = here.chips - 1 - p
        upsample(here.block(i, True))
        scatter.to_sibling(i).start()
        upsample(here.block(i, False))

        @pl.when(i > 0)
        def _():
            scatter.pass_on(i)

        return carry

    load_up.wait()
    lax.fori_loop(0, here.chips, upsample_step, 0)
    weights.exchange()
    scatter.arrive()

    step = min(64, rows)

    def total_step(q, carry):
        start = q * step
        up[pl.ds(pl.multiple_of(16 + start, 16), step)] = scatter.total((start, step)).astype(BF16)
        return carry

    lax.fori_loop(0, rows // step, total_step, 0)

    up_send = remote(up.at[pl.ds(rows, 16)], halo_low, edge_send.at[2], edge_recv.at[2], later)
    down_send = remote(up.at[pl.ds(16, 16)], halo_high, edge_send.at[3], edge_recv.at[3], earlier)

    @pl.when(not_end)
    def _():
        up_send.start()

    @pl.when(not_begin)
    def _():
        down_send.start()

    weights.pass_on()

    @pl.when(begin)
    def _():
        halo_low[...] = jnp.zeros(halo_low.shape, BF16)

    @pl.when(end)
    def _():
        halo_high[...] = jnp.zeros(halo_high.shape, BF16)

    alpha_one, alpha_two = alpha[0:1], alpha[1:2]

    def act_step(q, carry):
        start = q * step
        source = pl.ds(pl.multiple_of(16 + start, 16), step)
        target = pl.ds(pl.multiple_of(8 + start, 8), step)
        for phase in range(4):
            block = up[source, phase * mid : (phase + 1) * mid].astype(F32)
            acts[phase, target] = snake_act(block, alpha_one)
        return carry

    lax.fori_loop(0, rows // step, act_step, 0)

    @pl.when(not_begin)
    def _():
        up_send.wait_recv()

    @pl.when(not_end)
    def _():
        down_send.wait_recv()

    for phase in range(4):
        cols = slice(phase * mid, (phase + 1) * mid)
        acts[phase, pl.ds(0, 8)] = snake_act(halo_low[:, cols].astype(F32)[8:16], alpha_one)
        acts[phase, pl.ds(rows + 8, 8)] = snake_act(halo_high[:, cols].astype(F32)[0:8], alpha_one)

    length = rows + 16

    def prepare(befores, afters):
        for phase in range(4):
            block = acts[phase]
            taps[phase] = block.astype(BF16)
            if phase in befores:
                taps[4 + befores.index(phase)] = pltpu.roll(block, 1, 0).astype(BF16)
            if phase in afters:
                taps[4 + len(befores) + afters.index(phase)] = pltpu.roll(block, length - 1, 0).astype(BF16)

    chunk = 256 if mid % 256 == 0 else mid
    prepare((1, 2, 3), (0, 1, 2))
    line = lax.broadcasted_iota(jnp.int32, (length, 1), 0)
    outside = (begin & (line < 8)) | (end & (line >= rows + 8))
    row_mask = jnp.where(outside, 0.0, 1.0)

    load.wait()

    def dilated_step(q, carry):
        cols = pl.ds(pl.multiple_of(q * chunk, chunk), chunk)
        row = alpha[1:2, cols]
        for phase in range(4):
            low = 4 + phase if phase < 3 else 0
            high = 3 if phase == 0 else 6 + phase
            inner = dot(taps[low], w_dilated[0, :, cols])
            inner = inner + dot(taps[phase], w_dilated[1, :, cols])
            inner = inner + dot(taps[high], w_dilated[2, :, cols])
            acts[phase, :, cols] = snake_act(inner, row) * row_mask
        return carry

    lax.fori_loop(0, mid // chunk, dilated_step, 0)
    prepare((3,), (0,))
    weights.finish()

    def plain_step(q, carry):
        cols = pl.ds(pl.multiple_of(q * chunk, chunk), chunk)
        for phase in range(4):
            low = 4 if phase == 0 else phase - 1
            high = 5 if phase == 3 else phase + 1
            outer = dot(taps[low], w_plain[0, :, cols])
            outer = outer + dot(taps[phase], w_plain[1, :, cols])
            outer = outer + dot(taps[high], w_plain[2, :, cols])
            base = up[pl.ds(16, rows), pl.ds(pl.multiple_of(phase * mid + q * chunk, chunk), chunk)]
            result = base.astype(F32) + outer[8 : 8 + rows]
            for lane in range(chunk // 128):
                woven[phase, :, pl.ds(pl.multiple_of(q * chunk + lane * 128, 128), 128)] = result[
                    :, lane * 128 : (lane + 1) * 128
                ]
        return carry

    lax.fori_loop(0, mid // chunk, plain_step, 0)

    def weave_step(q, carry):
        part = [woven[phase, pl.ds(pl.multiple_of(q * 16, 16), 16)] for phase in range(4)]
        out[pl.ds(pl.multiple_of(q * 64, 64), 64)] = jnp.stack(part, 1).reshape(64, mid).astype(BF16)
        return carry

    lax.fori_loop(0, rows // 16, weave_step, 0)

    @pl.when(not_last)
    def _():
        mel_up.wait_send()

    @pl.when(not_first)
    def _():
        mel_down.wait_send()

    @pl.when(not_end)
    def _():
        up_send.wait_send()

    @pl.when(not_begin)
    def _():
        down_send.wait_send()

    scatter.finish()


def section(mel, w_prelude, w_upsample, snake_alpha, w_dilated, w_plain):
    n = lax.axis_size("sub")
    chips = n // 2
    total_rows, bands = mel.shape
    rows = total_rows // n
    mid = w_upsample.shape[2]
    wide = 4 * mid
    return pl.pallas_call(
        section_kernel,
        out_shape=jax.ShapeDtypeStruct((4 * rows, mid), BF16),
        in_specs=[
            pl.BlockSpec(memory_space=space) for space in [VMEM] * 2 + [pl.ANY, VMEM] + [pl.ANY] * 2
        ],
        out_specs=pl.BlockSpec(memory_space=VMEM),
        scratch_shapes=[
            VMEM((total_rows + 32, bands), F32),
            VMEM((total_rows + 16, w_prelude.shape[2]), F32),
            VMEM((total_rows, wide), BF16),
            VMEM((chips, rows, wide), BF16),
            VMEM((chips, rows, wide), BF16),
            VMEM((rows + 16, wide), BF16),
            VMEM((10, rows + 16, mid), BF16),
            VMEM((4, rows + 16, mid), F32),
            VMEM((4, rows, mid), F32),
            VMEM((16, wide), BF16),
            VMEM((16, wide), BF16),
            VMEM(w_dilated.shape, BF16),
            VMEM(w_dilated.shape, BF16),
            VMEM(w_upsample.shape, BF16),
            DMA((4, chips)),
            DMA((6, chips)),
            DMA((4,)),
            DMA((4,)),
            DMA((2,)),
        ],
        compiler_params=pltpu.CompilerParams(
            collective_id=1, has_side_effects=True, vmem_limit_bytes=58 * 2**20
        ),
        cost_estimate=pl.CostEstimate(flops=60 * 10**9, bytes_accessed=16 * 2**20, transcendentals=0),
        name="section",
    )(mel, w_prelude, w_upsample, snake_alpha, w_dilated, w_plain)


def body(
    frames, modulation, w_project, w_heads_out, w_up, w_down, w_velocity, noisy_mel, w_prelude,
    w_upsample, snake_alpha, w_dilated, w_plain,
):
    mel_next, dilated_all = layer(
        frames, modulation, w_project, w_heads_out, w_up, w_down, w_velocity.T, noisy_mel, w_dilated
    )
    section_out = section(
        mel_next, jnp.swapaxes(w_prelude, 1, 2), w_upsample, snake_alpha, dilated_all, w_plain
    )
    return (mel_next, section_out)


def solution(mesh):
    in_specs = (
        P(("tm", "sub"), None),
        P(),
        P(None, None, "sub"),
        P("sub", None),
        P(None, "sub"),
        P("sub", None),
        P(),
        P("tm", None),
        P(None, "sub", None),
        P(None, "sub", None),
        P(),
        P(None, "sub", None),
        P(None, "sub", None),
    )
    out_specs = (P("tm", None), P(("tm", "sub"), None))
    return jax.shard_map(body, mesh=mesh, in_specs=in_specs, out_specs=out_specs, check_vma=False)
```
